512 devices in a mesh: grp: 64 (over z, x_lo, core), freq: 8 (over y, x_hi).
Axes of the slice: x: 4 (x_hi: 2, x_lo: 2; x = x_hi * 2 + x_lo), y: 4, z: 16, core: 2. Of those that a mesh axis runs over, the one named last changes fastest.
Arguments:
- spectra: bfloat16 [8192, 8, 2, 1024], P('grp', None, None, 'freq')
- pairing: int32 [2, 64], replicated, may hold values from 0 to 63, as said below
Outputs:
- correlations: float32 [2, 4096, 128, 256], P(None, ('grp', 'freq'))
The draws below stay inside these ranges and needn't reach their ends.
Inputs may be any that keep to these rules, and one draw needn't show every extreme that they name: In every round each group's partner is another group, and pairing[r, pairing[r, g]] = g.
All inputs are finite; a program needn't handle non-finite values.
Results may differ from the reference program's by a relative error of at most 0.0055.
Values may be sent and summed in bfloat16 or wider, within the bound.
A program may use at most 64 MiB of HBM per device.

```python
import math
import jax
import jax.numpy as jnp
from jax import lax

GROUP_CHANNELS = 128
WIN = 8
LAGS = 256
VIRTUAL_SOURCES = 64
ROUNDS = 2
GROUPS = 64
CHANNELS = 8192
FREQ = 1024
SOURCES = 4096


def draw_spectra(key, part):
    key = jax.random.fold_in(key, 11)
    key_base, key_chan, key_rough, key_window = jax.random.split(key, 4)
    shape = (CHANNELS, WIN, 2, FREQ)
    base = jax.random.normal(key_base, shape, jnp.float32)
    slope = 2.0
    chan_scale = jnp.exp(jax.random.uniform(key_chan, (CHANNELS, 1, 1, 1), jnp.float32) * math.log(10.0))
    rough = jax.random.uniform(key_rough, (1, 1, 1, FREQ), jnp.float32, 0.5, 1.5)
    window_scale = jax.random.uniform(key_window, (CHANNELS, WIN, 1, 1), jnp.float32, 0.5, 1.5)
    positions = jnp.arange(FREQ, dtype=jnp.float32) / FREQ
    freq_scale = (1.0 + slope * positions)[None, None, None, :] * rough
    return (base * chan_scale * window_scale * freq_scale).astype(jnp.bfloat16)


def draw_pairing(key, part):
    key = jax.random.fold_in(key, 23)
    rows = []
    for which_round in range(ROUNDS):
        order = jax.random.permutation(jax.random.fold_in(key, which_round), GROUPS).astype(jnp.int32)
        mates = jnp.zeros((GROUPS,), jnp.int32)
        mates = mates.at[order[0::2]].set(order[1::2]).at[order[1::2]].set(order[0::2])
        rows.append(mates)
    return jnp.stack(rows)


def setup_inputs(seed: int = 0) -> dict:
    keys = jax.random.split(jax.random.key(seed), 3)
    spectra = draw_spectra(jax.random.fold_in(keys[2], 71), 0)
    pairing = draw_pairing(jax.random.fold_in(keys[2], 71), 0)
    return {"spectra": spectra, "pairing": pairing}


def lag_table(first_bin, bin_count, freq_total):
    bins = first_bin + jnp.arange(bin_count, dtype=jnp.int32)
    shifts = jnp.arange(LAGS, dtype=jnp.int32) - LAGS // 2
    phase_int = bins[:, None] * shifts[None, :] % (2 * freq_total)
    theta = phase_int.astype(jnp.float32) * (math.pi / freq_total)
    weights = jnp.where(bins == 0, 1.0, 2.0).astype(jnp.float32) / (2.0 * freq_total)
    return jnp.stack([weights[:, None] * jnp.cos(theta), -weights[:, None] * jnp.sin(theta)]).astype(jnp.bfloat16)

def normalise(spectra):
    energy = lax.optimization_barrier(jnp.sum(jnp.square(spectra.astype(jnp.float32)), axis=(1, 2, 3)))
    scaling = lax.rsqrt(energy / (WIN * 2 * FREQ) + 1e-06)
    return (spectra.astype(jnp.float32) * scaling[:, None, None, None]).astype(jnp.bfloat16)

def cross_spectra(source_channels, partner):
    src_count, win_count, two_parts, bins = source_channels.shape
    real_left = source_channels.reshape(src_count, win_count * 2, bins).astype(jnp.float32)
    imag_left = jnp.stack([source_channels[:, :, 1], -source_channels[:, :, 0]], axis=2).reshape(src_count, win_count * 2, bins).astype(jnp.float32)
    right = partner.reshape(partner.shape[0], win_count * 2, bins).astype(jnp.float32)
    real_part = (jnp.einsum('skf,ckf->scf', real_left, right) / win_count).astype(jnp.bfloat16)
    imag_part = (jnp.einsum('skf,ckf->scf', imag_left, right) / win_count).astype(jnp.bfloat16)
    return jnp.stack([real_part, imag_part], axis=2)

def reference(spectra, pairing):
    whitened_spectra = normalise(spectra)
    block_list = whitened_spectra.reshape(GROUPS, GROUP_CHANNELS, WIN, 2, FREQ)
    table = lag_table(0, FREQ, FREQ).astype(jnp.float32)
    owners = jnp.tile(jnp.arange(GROUPS, dtype=jnp.int32), ROUNDS)
    mates = pairing.reshape(-1).astype(jnp.int32)

    def one_pair(pair_indices):
        source_channels = block_list[pair_indices[0]][::GROUP_CHANNELS // VIRTUAL_SOURCES]
        spectrum = cross_spectra(source_channels, block_list[pair_indices[1]])
        return jnp.einsum('scpf,pfl->scl', spectrum.astype(jnp.float32), table)
    result = lax.map(one_pair, jnp.stack([owners, mates], axis=1))
    return result.reshape(ROUNDS, SOURCES, GROUP_CHANNELS, LAGS)
```

```python
import functools
import math

import jax
import jax.numpy as jnp
import numpy as np
from jax import lax
from jax.experimental import pallas as pl
from jax.experimental.pallas import tpu as pltpu
from jax.sharding import PartitionSpec as P

LAGS = 256
VIRTUAL_SOURCES = 64
ROUNDS = 2
MESH = pl.DeviceIdType.MESH
CHUNKS = 4


def lag_table(freq_total):
    bins = np.arange(freq_total)
    shifts = np.arange(LAGS) - LAGS // 2
    theta = (bins[:, None] * shifts[None, :] % (2 * freq_total)) * (math.pi / freq_total)
    weights = np.where(bins == 0, 1.0, 2.0) / (2.0 * freq_total)
    return np.stack([weights[:, None] * np.cos(theta), -weights[:, None] * np.sin(theta)])


def spread_table(sources, k):
    table = np.zeros((sources, k, sources, 2, 16, k), np.float32)
    for s in range(sources):
        for w in range(k // 2):
            table[s, 2 * w, s, 0, :, 2 * w] = 1.0
            table[s, 2 * w + 1, s, 0, :, 2 * w + 1] = 1.0
            table[s, 2 * w + 1, s, 1, :, 2 * w] = 1.0
            table[s, 2 * w, s, 1, :, 2 * w + 1] = -1.0
    return table.reshape(sources * k, sources * 2 * 16 * k)


def exchange_kernel(
    depth, ring, denominator,
    pair, e_in, x, s2, blk, s2o,
    e_all, xn, s2n, mid, send,
    e_ss, e_rs, s_ss, s_rs, z_ss, z_rs, l_ss, l_rs, c_ss, c_rs, p_ss, p_rs, a_ss, a_rs,
):
    freqs = 2 * ring
    rows = x.shape[0] // depth
    g = lax.axis_index("grp")
    q = lax.axis_index("freq")
    z = lax.div(g, 4)
    quad = lax.rem(g, 4)
    lo = lax.div(quad, 2)
    core = lax.rem(quad, 2)
    y = lax.div(q, 2)
    hi = lax.rem(q, 2)
    up = lax.rem(y + 1, ring)
    down = lax.rem(y + ring - 1, ring)
    across = lax.rem(y + 2, ring)
    lo_dev = (z * 4 + (1 - lo) * 2 + core, q)
    core_dev = (z * 4 + lo * 2 + (1 - core), q)
    mate_dev = (g, y * 2 + 1 - hi)
    up_dev = (g, up * 2 + hi)
    down_dev = (g, down * 2 + hi)

    def z_dev(zt):
        return (zt * 4 + quad, q)

    def copy(src, dst, ss, rs, dev):
        return pltpu.make_async_remote_copy(
            src_ref=src, dst_ref=dst, send_sem=ss, recv_sem=rs, device_id=dev, device_id_type=MESH
        )

    def arrived(ref, sem):
        pltpu.make_async_copy(ref, ref, sem).wait()

    barrier = pltpu.get_barrier_semaphore()
    for d in range(1, depth):
        pl.semaphore_signal(barrier, inc=1, device_id=z_dev(lax.rem(z + d, depth)), device_id_type=MESH)
    for d in range(1, freqs):
        pl.semaphore_signal(barrier, inc=1, device_id=(g, lax.rem(q + d, freqs)), device_id_type=MESH)
    for dev in (lo_dev, core_dev):
        pl.semaphore_signal(barrier, inc=1, device_id=dev, device_id_type=MESH)
    pl.semaphore_wait(barrier, depth - 1 + freqs - 1 + 2)

    for d in range(1, freqs):
        copy(e_in, e_all.at[q], e_ss.at[d], e_rs.at[q], (g, lax.rem(q + d, freqs))).start()
    e_all[q] = e_in[...]
    for d in range(1, freqs):
        src = lax.rem(q + d, freqs)
        arrived(e_all.at[src], e_rs.at[src])
    total = e_all[0]
    for i in range(1, freqs):
        total = total + e_all[i]
    scale = lax.rsqrt(total / denominator + 1e-06)
    xn[...] = (x[...].astype(jnp.float32) * scale[0:1, :][None]).astype(jnp.bfloat16)

    def spread(d, carry):
        zt = lax.rem(z + d, depth)
        copy(xn.at[pl.ds(zt * rows, rows)], mid.at[g], z_ss.at[zt], z_rs.at[z], z_dev(zt)).start()
        return carry

    lax.fori_loop(1, depth, spread, 0)
    mid[g] = xn[pl.ds(z * rows, rows)]

    for i in range(freqs):
        s2n[i] = (s2[i].astype(jnp.float32) * scale[8 + i : 9 + i, :]).astype(jnp.bfloat16)
    for d in range(1, freqs):
        to = lax.rem(q + d, freqs)
        copy(s2n.at[to], s2o.at[q], s_ss.at[d], s_rs.at[q], (g, to)).start()
    own_s2 = pltpu.make_async_copy(s2n.at[q], s2o.at[q], s_ss.at[0])
    own_s2.start()

    def pass_on(d, carry):
        zs = lax.rem(z + depth - d, depth)
        slot = mid.at[zs * 4 + quad]

        @pl.when(d > 0)
        def _():
            arrived(slot, z_rs.at[zs])

        copy(slot, slot, l_ss.at[zs], l_rs.at[zs], lo_dev).start()
        copy(slot, slot, c_ss.at[0, zs], c_rs.at[0, zs], core_dev).start()
        return carry

    lax.fori_loop(0, depth, pass_on, 0)

    def pass_twice(d, carry):
        zs = lax.rem(z + depth - d, depth)
        slot = mid.at[zs * 4 + (1 - lo) * 2 + core]
        arrived(slot, l_rs.at[zs])
        copy(slot, slot, c_ss.at[1, zs], c_rs.at[1, zs], core_dev).start()
        return carry

    lax.fori_loop(0, depth, pass_twice, 0)

    def gathered(d, carry):
        zs = lax.rem(z + depth - d, depth)
        arrived(mid.at[zs * 4 + lo * 2 + 1 - core], c_rs.at[0, zs])
        arrived(mid.at[zs * 4 + (1 - lo) * 2 + 1 - core], c_rs.at[1, zs])
        return carry

    lax.fori_loop(0, depth, gathered, 0)

    def select(r):
        here = pl.ds(z * rows, rows)

        def step(d, carry):
            zt = lax.rem(z + d, depth)
            send[r, zt] = mid[pair[r, zt * 4 + quad]]
            copy(send.at[r, zt], blk.at[r, q, here], p_ss.at[r, zt], p_rs.at[r, z], z_dev(zt)).start()
            return carry

        lax.fori_loop(1, depth, step, 0)
        send[r, z] = mid[pair[r, z * 4 + quad]]
        pltpu.make_async_copy(send.at[r, z], blk.at[r, q, here], p_rs.at[r, z]).start()

    per_chunk = depth // CHUNKS
    span = per_chunk * rows
    half = span // 2

    def part(r, fb, j):
        return blk.at[r, fb, pl.ds(j * span, span)]

    def halves(r, fb, j, h):
        return blk.at[r, fb, pl.ds(j * span + h * half, half)]

    def first(r, j):
        for i in range(per_chunk):
            zm = j * per_chunk + i
            arrived(blk.at[r, q, pl.ds(zm * rows, rows)], p_rs.at[r, zm])
        own = part(r, q, j)
        copy(own, own, a_ss.at[r, j, 0], a_rs.at[r, j, 0], mate_dev).start()
        copy(own, own, a_ss.at[r, j, 1], a_rs.at[r, j, 1], up_dev).start()
        copy(own, own, a_ss.at[r, j, 3], a_rs.at[r, j, 3], down_dev).start()

    def second(r, j):
        mate = part(r, y * 2 + 1 - hi, j)
        arrived(mate, a_rs.at[r, j, 0])
        copy(mate, mate, a_ss.at[r, j, 2], a_rs.at[r, j, 2], up_dev).start()
        copy(mate, mate, a_ss.at[r, j, 4], a_rs.at[r, j, 4], down_dev).start()

    def third(r, j):
        for i in range(2):
            side = hi if i == 0 else 1 - hi
            arrived(part(r, down * 2 + side, j), a_rs.at[r, j, 1 + i])
            a = halves(r, down * 2 + side, j, 0)
            copy(a, a, a_ss.at[r, j, 5 + i], a_rs.at[r, j, 5 + i], up_dev).start()
            arrived(part(r, up * 2 + side, j), a_rs.at[r, j, 3 + i])
            b = halves(r, up * 2 + side, j, 1)
            copy(b, b, a_ss.at[r, j, 7 + i], a_rs.at[r, j, 7 + i], down_dev).start()

    def fourth(r, j):
        for i in range(2):
            side = hi if i == 0 else 1 - hi
            arrived(halves(r, across * 2 + side, j, 0), a_rs.at[r, j, 5 + i])
            arrived(halves(r, across * 2 + side, j, 1), a_rs.at[r, j, 7 + i])

    select(0)
    first(0, 0)
    first(0, 1)
    select(1)
    first(0, 2)
    first(0, 3)
    for j in range(CHUNKS):
        second(0, j)
    third(0, 0)
    third(0, 1)
    first(1, 0)
    third(0, 2)
    first(1, 1)
    third(0, 3)
    first(1, 2)
    first(1, 3)
    for j in range(CHUNKS):
        second(1, j)
    for j in range(CHUNKS):
        third(1, j)
    for r in range(ROUNDS):
        for j in range(CHUNKS):
            fourth(r, j)

    own_s2.wait()
    for d in range(1, freqs):
        to = lax.rem(q + d, freqs)
        arrived(s2o.at[to], s_rs.at[to])
        arrived(s2n.at[to], s_ss.at[d])
        arrived(e_in, e_ss.at[d])

    def sent(d, carry):
        zt = lax.rem(z + d, depth)

        @pl.when(d > 0)
        def _():
            arrived(mid.at[0], z_ss.at[zt])
            arrived(mid.at[0], p_ss.at[0, zt])
            arrived(mid.at[0], p_ss.at[1, zt])

        arrived(mid.at[0], l_ss.at[zt])
        arrived(mid.at[0], c_ss.at[0, zt])
        arrived(mid.at[0], c_ss.at[1, zt])
        return carry

    lax.fori_loop(0, depth, sent, 0)
    for r in range(ROUNDS):
        for j in range(CHUNKS):
            for i in range(5):
                arrived(part(r, 0, j), a_ss.at[r, j, i])
            for i in range(5, 9):
                arrived(halves(r, 0, j, 0), a_ss.at[r, j, i])


def exchange(mesh_shape, denominator, pairing, e_in, x, s2):
    freqs = mesh_shape["freq"]
    groups = mesh_shape["grp"]
    depth, ring = groups // 4, freqs // 2
    bins, k, channels = x.shape
    rows = bins // depth
    dma = pltpu.SemaphoreType.DMA
    vmem = pl.BlockSpec(memory_space=pltpu.VMEM)
    return pl.pallas_call(
        functools.partial(exchange_kernel, depth, ring, denominator),
        out_shape=(
            jax.ShapeDtypeStruct((ROUNDS, freqs, bins, k, channels), jnp.bfloat16),
            jax.ShapeDtypeStruct(s2.shape, jnp.bfloat16),
        ),
        in_specs=[pl.BlockSpec(memory_space=pltpu.SMEM), vmem, vmem, vmem],
        out_specs=(pl.BlockSpec(memory_space=pl.ANY), pl.BlockSpec(memory_space=pl.ANY)),
        scratch_shapes=[
            pltpu.VMEM((freqs,) + e_in.shape, jnp.float32),
            pltpu.VMEM(x.shape, jnp.bfloat16),
            pltpu.VMEM(s2.shape, jnp.bfloat16),
            pltpu.VMEM((groups, rows, k, channels), jnp.bfloat16),
            pltpu.VMEM((ROUNDS, depth, rows, k, channels), jnp.bfloat16),
            dma((freqs,)), dma((freqs,)),
            dma((freqs,)), dma((freqs,)),
            dma((depth,)), dma((depth,)),
            dma((depth,)), dma((depth,)),
            dma((2, depth)), dma((2, depth)),
            dma((ROUNDS, depth)), dma((ROUNDS, depth)),
            dma((ROUNDS, CHUNKS, 9)), dma((ROUNDS, CHUNKS, 9)),
        ],
        compiler_params=pltpu.CompilerParams(
            collective_id=0, has_side_effects=True, vmem_limit_bytes=32 * 2**20
        ),
        name="exchange",
    )(pairing, e_in, x, s2)


def correlate_kernel(steps, windows, blk, s2, table, picks, out, w, spec, acc):
    step = pl.program_id(0)
    bins = s2.shape[1]
    tiles = bins // 16
    sources = w.shape[1] // 2
    wide = w.shape[3]
    row = lax.broadcasted_iota(jnp.int32, (16, wide), 0)
    col = lax.broadcasted_iota(jnp.int32, (16, wide), 1)
    mask = lax.div(col, wide // 16) == row
    for n in range(2 * sources):
        v = jnp.dot(s2[0], picks[:, n * wide : (n + 1) * wide], preferred_element_type=jnp.float32)
        v = jnp.where(mask[None], v.reshape(tiles, 16, wide), 0.0)
        w[:, n] = v.astype(jnp.bfloat16)
    for t in range(tiles):
        right = jnp.concatenate(
            [blk[r, 0, t * 16 : (t + 1) * 16].reshape(wide, -1) for r in range(ROUNDS)], axis=1
        )
        x = jnp.dot(w[t].reshape(-1, wide), right, preferred_element_type=jnp.float32)
        x = (x / windows).astype(jnp.bfloat16)
        for s in range(sources):
            for part in range(2):
                n = s * 2 + part
                spec[s, part * bins + t * 16 : part * bins + (t + 1) * 16, :] = x[n * 16 : (n + 1) * 16]

    @pl.when(step == 0)
    def _():
        for s in range(sources):
            acc[s] = jnp.dot(table[0], spec[s], preferred_element_type=jnp.float32)

    @pl.when(step > 0)
    def _():
        for s in range(sources):
            acc[s] += jnp.dot(table[0], spec[s], preferred_element_type=jnp.float32)

    @pl.when(step == steps - 1)
    def _():
        channels = out.shape[2]
        for s in range(sources):
            for r in range(ROUNDS):
                out[r, s] = acc[s, :, r * channels : (r + 1) * channels].T


def correlate(windows, sources, blk, s2, table, picks):
    rounds, freqs, bins, k, channels = blk.shape
    wide = 16 * k
    return pl.pallas_call(
        functools.partial(correlate_kernel, freqs, windows),
        out_shape=jax.ShapeDtypeStruct((rounds, sources, channels, LAGS), jnp.float32),
        grid=(freqs,),
        in_specs=[
            pl.BlockSpec((rounds, 1, bins, k, channels), lambda i: (0, i, 0, 0, 0)),
            pl.BlockSpec((1,) + s2.shape[1:], lambda i: (i, 0, 0)),
            pl.BlockSpec((1,) + table.shape[1:], lambda i: (i, 0, 0)),
            pl.BlockSpec(picks.shape, lambda i: (0, 0)),
        ],
        out_specs=pl.BlockSpec((rounds, sources, channels, LAGS), lambda i: (0, 0, 0, 0)),
        scratch_shapes=[
            pltpu.VMEM((bins // 16, 2 * sources, 16, wide), jnp.bfloat16),
            pltpu.VMEM((sources, 2 * bins, rounds * channels), jnp.bfloat16),
            pltpu.VMEM((sources, LAGS, rounds * channels), jnp.float32),
        ],
        compiler_params=pltpu.CompilerParams(vmem_limit_bytes=40 * 2**20),
        name="correlate",
    )(blk, s2, table, picks)


def per_device(mesh_shape, spectra, pairing):
    channels, windows, parts, bins = spectra.shape
    freqs = mesh_shape["freq"]
    k = windows * parts
    own = VIRTUAL_SOURCES // freqs
    flat = spectra.reshape(channels, k, bins)
    energy = jnp.sum(jnp.square(flat.astype(jnp.float32)), axis=(1, 2))
    step = channels // VIRTUAL_SOURCES
    per_lane = jnp.repeat(energy[::step].reshape(freqs, own), k, axis=1)
    e_in = jnp.concatenate([jnp.broadcast_to(energy[None], (8, channels)), per_lane])
    x = flat.transpose(2, 1, 0)
    s2 = flat[::step].reshape(freqs, own * k, bins).transpose(0, 2, 1)
    table = lag_table(freqs * bins).reshape(2, freqs, bins, LAGS).transpose(1, 3, 0, 2)
    table = jnp.asarray(table.reshape(freqs, LAGS, 2 * bins), jnp.bfloat16)
    picks = jnp.asarray(spread_table(own, k), jnp.bfloat16)
    blk, s2o = exchange(mesh_shape, k * bins * freqs, pairing, e_in, x, s2)
    return correlate(windows, own, blk, s2o, table, picks)


def solution(mesh):
    placed = (P("grp", None, None, "freq"), P())
    return jax.shard_map(
        functools.partial(per_device, dict(mesh.shape)),
        mesh=mesh,
        in_specs=placed,
        out_specs=P(None, ("grp", "freq"), None, None),
        check_vma=False,
    )
```

```python
import functools
import math

import jax
import jax.numpy as jnp
import numpy as np
from jax import lax
from jax.experimental import pallas as pl
from jax.experimental.pallas import tpu as pltpu
from jax.sharding import PartitionSpec as P

LAGS = 256
VIRTUAL_SOURCES = 64
ROUNDS = 2
MESH = pl.DeviceIdType.MESH
PARTS = 4
BATCH = 4
Y_FIRST = ((0, 1), (1, 1), (2, 1))


def lag_table(freq_total):
    bins = np.arange(freq_total)
    shifts = np.arange(LAGS) - LAGS // 2
    theta = (bins[:, None] * shifts[None, :] % (2 * freq_total)) * (math.pi / freq_total)
    weights = np.where(bins == 0, 1.0, 2.0) / (2.0 * freq_total)
    return np.stack([weights[:, None] * np.cos(theta), -weights[:, None] * np.sin(theta)])


def spread_table(sources, k):
    table = np.zeros((sources, k, sources, 2, 16, k), np.float32)
    for s in range(sources):
        for w in range(k // 2):
            table[s, 2 * w, s, 0, :, 2 * w] = 1.0
            table[s, 2 * w + 1, s, 0, :, 2 * w + 1] = 1.0
            table[s, 2 * w + 1, s, 1, :, 2 * w] = 1.0
            table[s, 2 * w, s, 1, :, 2 * w + 1] = -1.0
    return table.reshape(sources * k, sources * 2 * 16 * k)


def kernel(
    depth, ring, windows,
    pair, x, s2, table, picks, out,
    e_own, e_all, xn, s2n, s2o, send, blk, w, spec, acc, *rest,
):
    mids = rest[:PARTS]
    (e_ss, e_rs, s_ss, s_rs, z_ss, z_rs, l_ss, l_rs, c_ss, c_rs, p_ss, p_rs, a_ss, a_rs) = rest[PARTS:]
    freqs = 2 * ring
    bins, k, channels = x.shape
    width = bins // PARTS
    rows = width // depth
    sources = out.shape[1]
    wide = 16 * k
    tiles = width // 16
    g = lax.axis_index("grp")
    q = lax.axis_index("freq")
    z = lax.div(g, 4)
    quad = lax.rem(g, 4)
    lo = lax.div(quad, 2)
    core = lax.rem(quad, 2)
    y = lax.div(q, 2)
    hi = lax.rem(q, 2)
    up = lax.rem(y + 1, ring)
    down = lax.rem(y + ring - 1, ring)
    across = lax.rem(y + 2, ring)
    lo_quad = (1 - lo) * 2 + core
    core_quad = lo * 2 + 1 - core
    far_quad = (1 - lo) * 2 + 1 - core
    lo_dev = (z * 4 + lo_quad, q)
    core_dev = (z * 4 + core_quad, q)
    mate = y * 2 + 1 - hi
    mate_dev = (g, mate)
    up_dev = (g, up * 2 + hi)
    down_dev = (g, down * 2 + hi)

    def z_dev(zt):
        return (zt * 4 + quad, q)

    def copy(src, dst, ss, rs, dev):
        pltpu.make_async_remote_copy(
            src_ref=src, dst_ref=dst, send_sem=ss, recv_sem=rs, device_id=dev, device_id_type=MESH
        ).start()

    def arrived(ref, sem):
        pltpu.make_async_copy(ref, ref, sem).wait()

    barrier = pltpu.get_barrier_semaphore()
    for d in range(1, depth):
        pl.semaphore_signal(barrier, inc=1, device_id=z_dev(lax.rem(z + d, depth)), device_id_type=MESH)
    for d in range(1, freqs):
        pl.semaphore_signal(barrier, inc=1, device_id=(g, lax.rem(q + d, freqs)), device_id_type=MESH)
    for dev in (lo_dev, core_dev):
        pl.semaphore_signal(barrier, inc=1, device_id=dev, device_id_type=MESH)

    def square_sum(i, total):
        v = x[pl.ds(i * 8, 8)].astype(jnp.float32)
        return total + jnp.sum(v * v, axis=0)

    total = lax.fori_loop(0, bins // 8, square_sum, jnp.zeros((k, channels), jnp.float32))
    e_own[0:8] = jnp.broadcast_to(jnp.sum(total, axis=0, keepdims=True), (8, channels))
    for i in range(freqs):
        v = s2[i].astype(jnp.float32)
        e_own[8 + i : 9 + i] = jnp.sum(v * v, axis=0, keepdims=True)
    lanes = e_own.shape[1]
    same = lax.div(lax.broadcasted_iota(jnp.int32, (lanes, lanes), 0), k) == lax.div(
        lax.broadcasted_iota(jnp.int32, (lanes, lanes), 1), k
    )
    e_own[8:] = jnp.dot(
        e_own[8:], same.astype(jnp.float32), precision=lax.Precision.HIGHEST, preferred_element_type=jnp.float32
    )

    pl.semaphore_wait(barrier, depth - 1 + freqs - 1 + 2)
    for d in range(1, freqs):
        copy(e_own, e_all.at[q], e_ss.at[d], e_rs.at[q], (g, lax.rem(q + d, freqs)))
    e_all[q] = e_own[...]
    for d in range(1, freqs):
        src = lax.rem(q + d, freqs)
        arrived(e_all.at[src], e_rs.at[src])
    total = e_all[0]
    for i in range(1, freqs):
        total = total + e_all[i]
    scale = lax.rsqrt(total / (k * bins * freqs) + 1e-06)

    def spread(a):
        part = pl.ds(a * width, width)
        xn[part] = (x[part].astype(jnp.float32) * scale[0:1, :][None]).astype(jnp.bfloat16)
        slot = pl.ds(quad * depth + z, 1)

        def step(d, carry):
            zt = lax.rem(z + d, depth)
            copy(
                xn.at[pl.ds(a * width + zt * rows, rows)], mids[a].at[quad * depth + z],
                z_ss.at[a, zt], z_rs.at[a, z], z_dev(zt),
            )
            return carry

        lax.fori_loop(1, depth, step, 0)
        mids[a][slot] = xn[pl.ds(a * width + z * rows, rows)][None]

    for a in range(PARTS):
        spread(a)
    for i in range(freqs):
        s2n[i] = (s2[i].astype(jnp.float32) * scale[8 + i : 9 + i, :]).astype(jnp.bfloat16)
    for d in range(1, freqs):
        to = lax.rem(q + d, freqs)
        copy(s2n.at[to], s2o.at[q], s_ss.at[d], s_rs.at[q], (g, to))
    s2o[q] = s2n[q]

    batches = depth // BATCH

    def run(a, quarter, b):
        return mids[a].at[pl.ds(quarter * depth + b * BATCH, BATCH)]

    def pass_on(a):
        def step(i, carry):
            b = lax.rem(lax.div(z, BATCH) + i, batches)

            def one(j, carry):
                zs = b * BATCH + j

                @pl.when(zs != z)
                def _():
                    arrived(mids[a].at[quad * depth + zs], z_rs.at[a, zs])

                return carry

            lax.fori_loop(0, BATCH, one, 0)
            part = run(a, quad, b)
            copy(part, part, l_ss.at[a, b], l_rs.at[a, b], lo_dev)
            copy(part, part, c_ss.at[a, 0, b], c_rs.at[a, 0, b], core_dev)
            return carry

        lax.fori_loop(0, batches, step, 0)

    def pass_twice(a):
        def step(i, carry):
            b = lax.rem(lax.div(z, BATCH) + i, batches)
            part = run(a, lo_quad, b)
            arrived(part, l_rs.at[a, b])
            copy(part, part, c_ss.at[a, 1, b], c_rs.at[a, 1, b], core_dev)
            return carry

        lax.fori_loop(0, batches, step, 0)

    def passed(a):
        for b in range(batches):
            arrived(run(a, core_quad, b), c_rs.at[a, 0, b])
            arrived(run(a, far_quad, b), c_rs.at[a, 1, b])

    def select(a, r):
        here = pl.ds(z * rows, rows)

        def wanted(zt):
            p = pair[r, zt * 4 + quad]
            return mids[a][lax.rem(p, 4) * depth + lax.div(p, 4)]

        def step(d, carry):
            zt = lax.rem(z + d, depth)
            send[a, r, zt] = wanted(zt)
            copy(send.at[a, r, zt], blk.at[a, q, r, here], p_ss.at[a, r, zt], p_rs.at[a, r, z], z_dev(zt))
            return carry

        lax.fori_loop(1, depth, step, 0)
        blk[a, q, r, here] = wanted(z)

    half = width // 2

    def block(a, r, fb):
        return blk.at[a, fb, r]

    def halves(a, r, fb, h):
        return blk.at[a, fb, r, pl.ds(h * half, half)]

    def ship(ref, a, r, i, dev):
        copy(ref, ref, a_ss.at[a, r, i], a_rs.at[a, r, i], dev)

    def first(a, r):
        def one(d, carry):
            zm = lax.rem(z + d, depth)
            arrived(blk.at[a, q, r, pl.ds(zm * rows, rows)], p_rs.at[a, r, zm])
            return carry

        lax.fori_loop(1, depth, one, 0)
        own = block(a, r, q)
        ship(own, a, r, 1, up_dev)
        ship(own, a, r, 3, down_dev)
        ship(own, a, r, 0, mate_dev)

    def second(a, r):
        if (a, r) in Y_FIRST:
            return
        other = block(a, r, mate)
        arrived(other, a_rs.at[a, r, 0])
        ship(other, a, r, 2, up_dev)
        ship(other, a, r, 4, down_dev)

    def third(a, r):
        for i in range(1 if (a, r) in Y_FIRST else 2):
            side = hi if i == 0 else 1 - hi
            low, high = down * 2 + side, up * 2 + side
            arrived(block(a, r, low), a_rs.at[a, r, 1 + i])
            ship(halves(a, r, low, 0), a, r, 5 + i, up_dev)
            arrived(block(a, r, high), a_rs.at[a, r, 3 + i])
            ship(halves(a, r, high, 1), a, r, 7 + i, down_dev)
            if (a, r) in Y_FIRST:
                ship(block(a, r, low), a, r, 2, mate_dev)
                ship(block(a, r, high), a, r, 4, mate_dev)

    def fourth(a, r):
        if (a, r) in Y_FIRST:
            arrived(halves(a, r, across * 2 + hi, 0), a_rs.at[a, r, 5])
            arrived(halves(a, r, across * 2 + hi, 1), a_rs.at[a, r, 7])
            ship(block(a, r, across * 2 + hi), a, r, 6, mate_dev)
            return
        for i in range(2):
            side = hi if i == 0 else 1 - hi
            arrived(halves(a, r, across * 2 + side, 0), a_rs.at[a, r, 5 + i])
            arrived(halves(a, r, across * 2 + side, 1), a_rs.at[a, r, 7 + i])

    def last(a, r):
        if (a, r) in Y_FIRST:
            arrived(block(a, r, mate), a_rs.at[a, r, 0])
            arrived(block(a, r, down * 2 + 1 - hi), a_rs.at[a, r, 2])
            arrived(block(a, r, up * 2 + 1 - hi), a_rs.at[a, r, 4])
            arrived(block(a, r, across * 2 + 1 - hi), a_rs.at[a, r, 6])

    def weights(a):
        row = lax.broadcasted_iota(jnp.int32, (16, wide), 0)
        col = lax.broadcasted_iota(jnp.int32, (16, wide), 1)
        mask = lax.div(col, k) == row

        def step(fb, carry):
            v = s2o[fb, a * width : (a + 1) * width, :]
            for n in range(2 * sources):
                u = jnp.dot(v, picks[:, n * wide : (n + 1) * wide], preferred_element_type=jnp.float32)
                w[a, fb, :, n] = jnp.where(mask[None], u.reshape(tiles, 16, wide), 0.0).astype(jnp.bfloat16)
            return carry

        lax.fori_loop(0, freqs, step, 0)

    def correlate(a):
        def step(fb, carry):
            for t in range(tiles):
                right = jnp.concatenate(
                    [blk[a, fb, r, t * 16 : (t + 1) * 16].reshape(wide, channels) for r in range(ROUNDS)], axis=1
                )
                v = jnp.dot(w[a, fb, t].reshape(2 * sources * 16, wide), right, preferred_element_type=jnp.float32)
                v = (v * (1.0 / windows)).astype(jnp.bfloat16)
                for s in range(sources):
                    for part in range(2):
                        n = s * 2 + part
                        at = pl.multiple_of(fb * (2 * width) + part * width + t * 16, 16)
                        spec[s, pl.ds(at, 16), :] = v[n * 16 : (n + 1) * 16]
            return carry

        lax.fori_loop(0, freqs, step, 0)
        span = 2 * width * freqs

        def lags(s, carry):
            v = jnp.dot(table[:, a * span : (a + 1) * span], spec[s], preferred_element_type=jnp.float32)
            if a > 0:
                v = v + acc[s]
            if a == PARTS - 1:
                for r in range(ROUNDS):
                    out[r, s] = v[:, r * channels : (r + 1) * channels].T
            else:
                acc[s] = v
            return carry

        lax.fori_loop(0, sources, lags, 0)

    turns = [(a, r) for a in range(PARTS) for r in range(ROUNDS)]
    pass_on(0)
    pass_twice(0)
    passed(0)
    select(*turns[0])
    for a in range(1, PARTS):
        pass_on(a)
        pass_twice(a)
        if a == 1:
            select(*turns[1])
        passed(a)
    for d in range(1, freqs):
        src = lax.rem(q + d, freqs)
        arrived(s2o.at[src], s_rs.at[src])
    ahead = 2
    for i in range(len(turns) + 3):
        if i < len(turns):
            first(*turns[i])
            if i + ahead < len(turns):
                select(*turns[i + ahead])
            second(*turns[i])
        if 0 <= i - 1 < len(turns):
            third(*turns[i - 1])
        if 0 <= i - 2 < len(turns):
            fourth(*turns[i - 2])
        if 0 <= i - 3 < len(turns):
            last(*turns[i - 3])
        if i < PARTS:
            weights(i)
        if i >= 3 and (i - 3) % ROUNDS == ROUNDS - 1:
            correlate((i - 3) // ROUNDS)

    for d in range(1, freqs):
        arrived(s2n.at[0], s_ss.at[d])
        arrived(e_own, e_ss.at[d])
    for a in range(PARTS):
        def sent(d, carry):
            zt = lax.rem(z + d, depth)
            arrived(mids[a].at[0], z_ss.at[a, zt])
            for r in range(ROUNDS):
                arrived(mids[a].at[0], p_ss.at[a, r, zt])
            return carry

        lax.fori_loop(1, depth, sent, 0)
        for b in range(batches):
            arrived(run(a, 0, b), l_ss.at[a, b])
            arrived(run(a, 0, b), c_ss.at[a, 0, b])
            arrived(run(a, 0, b), c_ss.at[a, 1, b])
        for r in range(ROUNDS):
            y_first = (a, r) in Y_FIRST
            for i in range(9):
                if y_first and i == 8:
                    continue
                whole = i < 5 or (y_first and i == 6)
                arrived(block(a, r, 0) if whole else halves(a, r, 0, 0), a_ss.at[a, r, i])


def per_device(mesh_shape, spectra, pairing):
    channels, windows, two, bins = spectra.shape
    freqs, groups = mesh_shape["freq"], mesh_shape["grp"]
    depth, ring = groups // 4, freqs // 2
    k = windows * two
    sources = VIRTUAL_SOURCES // freqs
    width = bins // PARTS
    rows = width // depth
    step = channels // VIRTUAL_SOURCES
    x = spectra.reshape(channels, k, bins).transpose(2, 1, 0)
    s2 = spectra.reshape(VIRTUAL_SOURCES, step, k, bins)[:, 0]
    s2 = lax.optimization_barrier(s2).reshape(freqs, sources * k, bins).transpose(0, 2, 1)
    table = lag_table(freqs * bins).reshape(2, freqs, PARTS, width, LAGS).transpose(4, 2, 1, 0, 3)
    table = jnp.asarray(table.reshape(LAGS, 2 * freqs * bins), jnp.bfloat16)
    picks = jnp.asarray(spread_table(sources, k), jnp.bfloat16)
    dma = pltpu.SemaphoreType.DMA
    vmem = pl.BlockSpec(memory_space=pltpu.VMEM)
    bf16, f32 = jnp.bfloat16, jnp.float32
    return pl.pallas_call(
        functools.partial(kernel, depth, ring, windows),
        out_shape=jax.ShapeDtypeStruct((ROUNDS, sources, channels, LAGS), f32),
        in_specs=[pl.BlockSpec(memory_space=pltpu.SMEM), vmem, vmem, vmem, vmem],
        out_specs=vmem,
        scratch_shapes=[
            pltpu.VMEM((8 + freqs, channels), f32),
            pltpu.VMEM((freqs, 8 + freqs, channels), f32),
            pltpu.VMEM(x.shape, bf16),
            pltpu.VMEM(s2.shape, bf16),
            pltpu.VMEM(s2.shape, bf16),
            pltpu.VMEM((PARTS, ROUNDS, depth, rows, k, channels), bf16),
            pltpu.VMEM((PARTS, freqs, ROUNDS, width, k, channels), bf16),
            pltpu.VMEM((PARTS, freqs, width // 16, 2 * sources, 16, 16 * k), bf16),
            pltpu.VMEM((sources, 2 * width * freqs, ROUNDS * channels), bf16),
            pltpu.VMEM((sources, LAGS, ROUNDS * channels), f32),
        ]
        + [pltpu.VMEM((groups, rows, k, channels), bf16)] * PARTS
        + [
            dma((freqs,)), dma((freqs,)),
            dma((freqs,)), dma((freqs,)),
            dma((PARTS, depth)), dma((PARTS, depth)),
            dma((PARTS, depth // BATCH)), dma((PARTS, depth // BATCH)),
            dma((PARTS, 2, depth // BATCH)), dma((PARTS, 2, depth // BATCH)),
            dma((PARTS, ROUNDS, depth)), dma((PARTS, ROUNDS, depth)),
            dma((PARTS, ROUNDS, 9)), dma((PARTS, ROUNDS, 9)),
        ],
        compiler_params=pltpu.CompilerParams(
            collective_id=0, has_side_effects=True, vmem_limit_bytes=48 * 2**20
        ),
        name="correlate_pairs",
    )(pairing, x, s2, table, picks)


def solution(mesh):
    placed = (P("grp", None, None, "freq"), P())
    return jax.shard_map(
        functools.partial(per_device, dict(mesh.shape)),
        mesh=mesh,
        in_specs=placed,
        out_specs=P(None, ("grp", "freq"), None, None),
        check_vma=False,
    )
```

```python
import functools
import math

import jax
import jax.numpy as jnp
import numpy as np
from jax import lax
from jax.experimental import pallas as pl
from jax.experimental.pallas import tpu as pltpu
from jax.sharding import PartitionSpec as P

LAGS = 256
VIRTUAL_SOURCES = 64
ROUNDS = 2
MESH = pl.DeviceIdType.MESH
PARTS = 4
BATCH = 4
Y_FIRST = ((0, 1), (1, 1), (2, 1))
ORDER = (
    ("E0", "Z1", "P0", "Z2", "E1", "Q0", "E2", "R0", "X0", "P1", "Q1", "R1", "X1", "O0", "E3", "W0")
    + ("F0", "X2", "P2", "Q2", "W1", "Z3", "F1", "S0", "X3", "R2", "F2", "X4", "S1", "T0", "P3", "Q3")
    + ("F3", "X5", "S2", "T1", "U0", "R3", "F4", "X6", "S3", "T2", "U1", "L0", "F5", "X7", "S4", "T3")
    + ("U2", "L1", "A0", "F6", "S5", "B0", "T4", "U3", "G0", "L2", "F7", "S6", "T5", "U4", "L3", "S7")
    + ("A1", "T6", "B1", "U5", "G1", "L4", "T7", "U6", "L5", "A2", "B2", "G2", "A3", "U7", "L6", "L7")
    + ("B3", "G3", "z0", "z1", "z2", "z3", "s0", "s1", "s2", "s3", "s4", "s5", "s6", "s7")
)


def lag_table(freq_total):
    bins = np.arange(freq_total)
    shifts = np.arange(LAGS) - LAGS // 2
    theta = (bins[:, None] * shifts[None, :] % (2 * freq_total)) * (math.pi / freq_total)
    weights = np.where(bins == 0, 1.0, 2.0) / (2.0 * freq_total)
    return np.stack([weights[:, None] * np.cos(theta), -weights[:, None] * np.sin(theta)])


def spread_table(sources, k):
    table = np.zeros((sources, k, sources, 2, 16, k), np.float32)
    for s in range(sources):
        for w in range(k // 2):
            table[s, 2 * w, s, 0, :, 2 * w] = 1.0
            table[s, 2 * w + 1, s, 0, :, 2 * w + 1] = 1.0
            table[s, 2 * w + 1, s, 1, :, 2 * w] = 1.0
            table[s, 2 * w, s, 1, :, 2 * w + 1] = -1.0
    return table.reshape(sources * k, sources * 2 * 16 * k)


def kernel(
    depth, ring, windows,
    pair, x, s2, table, picks, out,
    e_own, e_all, e_sum, e_grp, norm, s2o, send, blk, w, spec, acc, *rest,
):
    mids = rest[:PARTS]
    (e_ss, e_rs, g_ss, g_rs, t_ss, t_rs, s_ss, s_rs, z_ss, z_rs, l_ss, l_rs, c_ss, c_rs, p_ss, p_rs, a_ss, a_rs) = rest[PARTS:]
    freqs = 2 * ring
    bins, k, channels = x.shape
    width = bins // PARTS
    rows = width // depth
    sources = out.shape[1]
    wide = 16 * k
    tiles = width // 16
    g = lax.axis_index("grp")
    q = lax.axis_index("freq")
    z = lax.div(g, 4)
    quad = lax.rem(g, 4)
    lo = lax.div(quad, 2)
    core = lax.rem(quad, 2)
    y = lax.div(q, 2)
    hi = lax.rem(q, 2)
    up = lax.rem(y + 1, ring)
    down = lax.rem(y + ring - 1, ring)
    across = lax.rem(y + 2, ring)
    lo_quad = (1 - lo) * 2 + core
    core_quad = lo * 2 + 1 - core
    far_quad = (1 - lo) * 2 + 1 - core
    lo_dev = (z * 4 + lo_quad, q)
    core_dev = (z * 4 + core_quad, q)
    mate = y * 2 + 1 - hi
    mate_dev = (g, mate)
    up_dev = (g, up * 2 + hi)
    down_dev = (g, down * 2 + hi)

    def z_dev(zt):
        return (zt * 4 + quad, q)

    def place(i):
        d = lax.div(i + 1, 2)
        return lax.rem(z + i, depth)

    def copy(src, dst, ss, rs, dev):
        pltpu.make_async_remote_copy(
            src_ref=src, dst_ref=dst, send_sem=ss, recv_sem=rs, device_id=dev, device_id_type=MESH
        ).start()

    def arrived(ref, sem):
        pltpu.make_async_copy(ref, ref, sem).wait()

    barrier = pltpu.get_barrier_semaphore()
    for d in range(1, depth):
        pl.semaphore_signal(barrier, inc=1, device_id=z_dev(lax.rem(z + d, depth)), device_id_type=MESH)
    for d in range(1, freqs):
        pl.semaphore_signal(barrier, inc=1, device_id=(g, lax.rem(q + d, freqs)), device_id_type=MESH)
    for dev in (lo_dev, core_dev):
        pl.semaphore_signal(barrier, inc=1, device_id=dev, device_id_type=MESH)

    def square_sum(i, total):
        v = x[pl.ds(i * 8, 8)].astype(jnp.float32)
        return total + jnp.sum(v * v, axis=0)

    total = lax.fori_loop(0, bins // 8, square_sum, jnp.zeros((k, channels), jnp.float32))
    e_own[0:8] = jnp.broadcast_to(jnp.sum(total, axis=0, keepdims=True), (8, channels))
    for i in range(freqs):
        v = s2[i].astype(jnp.float32)
        e_own[8 + i : 9 + i] = jnp.sum(v * v, axis=0, keepdims=True)
    lanes = e_own.shape[1]
    same = lax.div(lax.broadcasted_iota(jnp.int32, (lanes, lanes), 0), k) == lax.div(
        lax.broadcasted_iota(jnp.int32, (lanes, lanes), 1), k
    )
    e_own[8:] = jnp.dot(
        e_own[8:], same.astype(jnp.float32), precision=lax.Precision.HIGHEST, preferred_element_type=jnp.float32
    )

    pl.semaphore_wait(barrier, depth - 1 + freqs - 1 + 2)

    def spread(a):
        def step(i, carry):
            zt = place(i)
            copy(
                x.at[pl.ds(a * width + zt * rows, rows)], mids[a].at[quad * depth + z],
                z_ss.at[a, zt], z_rs.at[a, z], z_dev(zt),
            )
            return carry

        lax.fori_loop(1, depth, step, 0)
        mids[a][pl.ds(quad * depth + z, 1)] = x[pl.ds(a * width + z * rows, rows)][None]

    spread(0)
    for d in range(1, freqs):
        to = lax.rem(q + d, freqs)
        copy(e_own, e_all.at[q], e_ss.at[d], e_rs.at[q], (g, to))
    e_all[q] = e_own[...]
    for d in range(1, freqs):
        to = lax.rem(q + d, freqs)
        copy(s2.at[to], s2o.at[q], s_ss.at[d], s_rs.at[q], (g, to))
    s2o[q] = s2[q]

    def energy_run(quarter):
        return e_grp.at[pl.ds(quarter * depth, depth)]

    def energies(step):
        if step == 0:
            for d in range(1, freqs):
                src = lax.rem(q + d, freqs)
                arrived(e_all.at[src], e_rs.at[src])
            total = e_all[0]
            for i in range(1, freqs):
                total = total + e_all[i]
            e_sum[...] = total
            e_grp[quad * depth + z] = total[0:8]

            def one(i, carry):
                zt = place(i)
                copy(e_sum.at[pl.ds(0, 8)], e_grp.at[quad * depth + z], g_ss.at[zt], g_rs.at[z], z_dev(zt))
                return carry

            lax.fori_loop(1, depth, one, 0)
        if step == 1:
            def one(d, carry):
                zs = lax.rem(z + d, depth)
                arrived(e_grp.at[quad * depth + zs], g_rs.at[zs])
                return carry

            lax.fori_loop(1, depth, one, 0)
            copy(energy_run(quad), energy_run(quad), t_ss.at[0], t_rs.at[0], lo_dev)
            copy(energy_run(quad), energy_run(quad), t_ss.at[1], t_rs.at[1], core_dev)
        if step == 2:
            arrived(energy_run(lo_quad), t_rs.at[0])
            copy(energy_run(lo_quad), energy_run(lo_quad), t_ss.at[2], t_rs.at[2], core_dev)
        if step == 3:
            arrived(energy_run(core_quad), t_rs.at[1])
            arrived(energy_run(far_quad), t_rs.at[2])
            count = k * bins * freqs
            for r in range(ROUNDS):
                p = pair[r, g]
                norm[r] = lax.rsqrt(e_grp[lax.rem(p, 4) * depth + lax.div(p, 4)] / count + 1e-06)
            own = e_sum[pl.ds(8 + q, 1)]
            norm[ROUNDS] = jnp.broadcast_to(lax.rsqrt(own / count + 1e-06), (8, channels))

    batches = depth // BATCH

    def run(a, quarter, b):
        return mids[a].at[pl.ds(quarter * depth + b * BATCH, BATCH)]

    def pass_on(a):
        def step(i, carry):
            b = lax.rem(lax.div(z, BATCH) + i, batches)

            def one(j, carry):
                zs = b * BATCH + j

                @pl.when(zs != z)
                def _():
                    arrived(mids[a].at[quad * depth + zs], z_rs.at[a, zs])

                return carry

            lax.fori_loop(0, BATCH, one, 0)
            part = run(a, quad, b)
            copy(part, part, l_ss.at[a, b], l_rs.at[a, b], lo_dev)
            copy(part, part, c_ss.at[a, 0, b], c_rs.at[a, 0, b], core_dev)
            return carry

        lax.fori_loop(0, batches, step, 0)

    def pass_twice(a):
        def step(i, carry):
            b = lax.rem(lax.div(z, BATCH) + i, batches)
            part = run(a, lo_quad, b)
            arrived(part, l_rs.at[a, b])
            copy(part, part, c_ss.at[a, 1, b], c_rs.at[a, 1, b], core_dev)
            return carry

        lax.fori_loop(0, batches, step, 0)

    def passed(a):
        for b in range(batches):
            arrived(run(a, core_quad, b), c_rs.at[a, 0, b])
            arrived(run(a, far_quad, b), c_rs.at[a, 1, b])

    def select(a, r):
        here = pl.ds(z * rows, rows)

        def wanted(zt):
            p = pair[r, zt * 4 + quad]
            return mids[a][lax.rem(p, 4) * depth + lax.div(p, 4)]

        def step(i, carry):
            zt = place(i)
            send[a, r, zt] = wanted(zt)
            copy(send.at[a, r, zt], blk.at[a, q, r, here], p_ss.at[a, r, zt], p_rs.at[a, r, z], z_dev(zt))
            return carry

        lax.fori_loop(1, depth, step, 0)
        blk[a, q, r, here] = wanted(z)

    half = width // 2

    def block(a, r, fb):
        return blk.at[a, fb, r]

    def halves(a, r, fb, h):
        return blk.at[a, fb, r, pl.ds(h * half, half)]

    def ship(ref, a, r, i, dev):
        copy(ref, ref, a_ss.at[a, r, i], a_rs.at[a, r, i], dev)

    def first(a, r):
        def one(d, carry):
            zm = lax.rem(z + d, depth)
            arrived(blk.at[a, q, r, pl.ds(zm * rows, rows)], p_rs.at[a, r, zm])
            return carry

        lax.fori_loop(1, depth, one, 0)
        own = block(a, r, q)
        ship(own, a, r, 1, up_dev)
        ship(own, a, r, 3, down_dev)
        ship(own, a, r, 0, mate_dev)

    def second(a, r):
        if (a, r) in Y_FIRST:
            return
        other = block(a, r, mate)
        arrived(other, a_rs.at[a, r, 0])
        ship(other, a, r, 2, up_dev)
        ship(other, a, r, 4, down_dev)

    def third(a, r):
        for i in range(1 if (a, r) in Y_FIRST else 2):
            side = hi if i == 0 else 1 - hi
            low, high = down * 2 + side, up * 2 + side
            arrived(block(a, r, low), a_rs.at[a, r, 1 + i])
            ship(halves(a, r, low, 0), a, r, 5 + i, up_dev)
            arrived(block(a, r, high), a_rs.at[a, r, 3 + i])
            ship(halves(a, r, high, 1), a, r, 7 + i, down_dev)
            if (a, r) in Y_FIRST:
                ship(block(a, r, low), a, r, 2, mate_dev)
                ship(block(a, r, high), a, r, 4, mate_dev)

    def fourth(a, r):
        if (a, r) in Y_FIRST:
            arrived(halves(a, r, across * 2 + hi, 0), a_rs.at[a, r, 5])
            arrived(halves(a, r, across * 2 + hi, 1), a_rs.at[a, r, 7])
            ship(block(a, r, across * 2 + hi), a, r, 6, mate_dev)
            return
        for i in range(2):
            side = hi if i == 0 else 1 - hi
            arrived(halves(a, r, across * 2 + side, 0), a_rs.at[a, r, 5 + i])
            arrived(halves(a, r, across * 2 + side, 1), a_rs.at[a, r, 7 + i])

    def last(a, r):
        if (a, r) in Y_FIRST:
            arrived(block(a, r, mate), a_rs.at[a, r, 0])
            arrived(block(a, r, down * 2 + 1 - hi), a_rs.at[a, r, 2])
            arrived(block(a, r, up * 2 + 1 - hi), a_rs.at[a, r, 4])
            arrived(block(a, r, across * 2 + 1 - hi), a_rs.at[a, r, 6])

    def weights(part):
        row = lax.broadcasted_iota(jnp.int32, (16, wide), 0)
        col = lax.broadcasted_iota(jnp.int32, (16, wide), 1)
        mask = lax.div(col, k) == row
        near = freqs // 2

        def step(i, carry):
            at = pl.ds(i * near, near)
            v = s2o[at].astype(jnp.float32) * norm[ROUNDS, 0:1][None]
            v = v.astype(jnp.bfloat16).reshape(near * bins, sources * k)
            for n in range(part * sources, (part + 1) * sources):
                u = jnp.dot(v, picks[:, n * wide : (n + 1) * wide], preferred_element_type=jnp.float32)
                u = jnp.where(mask[None], u.reshape(near * bins // 16, 16, wide), 0.0).astype(jnp.bfloat16)
                w[pl.ds(i * near * bins // 16, near * bins // 16), n] = u
            return carry

        lax.fori_loop(0, freqs // near, step, 0)

    def spectra(a, row):
        def step(side, carry):
            fb = row * 2 + side
            for t in range(tiles):
                right = jnp.concatenate(
                    [
                        (blk[a, fb, r, t * 16 : (t + 1) * 16].astype(jnp.float32) * norm[r, 0:1][None])
                        .astype(jnp.bfloat16)
                        .reshape(wide, channels)
                        for r in range(ROUNDS)
                    ],
                    axis=1,
                )
                left = w[fb * (bins // 16) + a * tiles + t].reshape(2 * sources * 16, wide)
                v = jnp.dot(left, right, preferred_element_type=jnp.float32)
                v = (v * (1.0 / windows)).astype(jnp.bfloat16)
                for s in range(sources):
                    for part in range(2):
                        n = s * 2 + part
                        at = pl.multiple_of(fb * (2 * width) + part * width + t * 16, 16)
                        spec[s, pl.ds(at, 16), :] = v[n * 16 : (n + 1) * 16]
            return carry

        lax.fori_loop(0, 2, step, 0)

    def near_spectra(a):
        for row in (y, up, down):
            spectra(a, row)

    def lags_of(a):
        span = 2 * width * freqs

        def lags(s, carry):
            v = jnp.dot(table[:, a * span : (a + 1) * span], spec[s], preferred_element_type=jnp.float32)
            if a > 0:
                v = v + acc[s]
            if a == PARTS - 1:
                for r in range(ROUNDS):
                    out[r, s] = v[:, r * channels : (r + 1) * channels].T
            else:
                acc[s] = v
            return carry

        lax.fori_loop(0, sources, lags, 0)

    turns = [(a, r) for a in range(PARTS) for r in range(ROUNDS)]

    def spread_sent(a):
        def one(d, carry):
            arrived(mids[a].at[0], z_ss.at[a, lax.rem(z + d, depth)])
            return carry

        lax.fori_loop(1, depth, one, 0)

    def select_sent(a, r):
        def one(d, carry):
            arrived(mids[a].at[0], p_ss.at[a, r, lax.rem(z + d, depth)])
            return carry

        lax.fori_loop(1, depth, one, 0)

    def sources_here():
        for d in range(1, freqs):
            src = lax.rem(q + d, freqs)
            arrived(s2o.at[src], s_rs.at[src])

    names = {
        "z": lambda a: spread_sent(a),
        "s": lambda t: select_sent(*turns[t]),
        "Z": lambda a: spread(a),
        "P": lambda a: pass_on(a),
        "Q": lambda a: pass_twice(a),
        "R": lambda a: passed(a),
        "X": lambda t: select(*turns[t]),
        "F": lambda t: first(*turns[t]),
        "S": lambda t: second(*turns[t]),
        "T": lambda t: third(*turns[t]),
        "U": lambda t: fourth(*turns[t]),
        "L": lambda t: last(*turns[t]),
        "O": lambda a: sources_here(),
        "W": lambda a: weights(a),
        "A": lambda a: near_spectra(a),
        "B": lambda a: spectra(a, across),
        "G": lambda a: lags_of(a),
        "E": lambda a: energies(a),
    }
    for name in ORDER:
        names[name[0]](int(name[1]))

    for d in range(1, freqs):
        arrived(s2.at[0], s_ss.at[d])
        arrived(e_own, e_ss.at[d])

    def energy_sent(d, carry):
        arrived(e_grp.at[0], g_ss.at[lax.rem(z + d, depth)])
        return carry

    lax.fori_loop(1, depth, energy_sent, 0)
    for i in range(3):
        arrived(energy_run(0), t_ss.at[i])
    for a in range(PARTS):
        for b in range(batches):
            arrived(run(a, 0, b), l_ss.at[a, b])
            arrived(run(a, 0, b), c_ss.at[a, 0, b])
            arrived(run(a, 0, b), c_ss.at[a, 1, b])
        for r in range(ROUNDS):
            y_first = (a, r) in Y_FIRST
            for i in range(9):
                if y_first and i == 8:
                    continue
                whole = i < 5 or (y_first and i == 6)
                arrived(block(a, r, 0) if whole else halves(a, r, 0, 0), a_ss.at[a, r, i])


def per_device(mesh_shape, spectra, pairing):
    channels, windows, two, bins = spectra.shape
    freqs, groups = mesh_shape["freq"], mesh_shape["grp"]
    depth, ring = groups // 4, freqs // 2
    k = windows * two
    sources = VIRTUAL_SOURCES // freqs
    width = bins // PARTS
    rows = width // depth
    step = channels // VIRTUAL_SOURCES
    x = spectra.reshape(channels, k, bins).transpose(2, 1, 0)
    s2 = spectra.reshape(VIRTUAL_SOURCES, step, k, bins)[:, 0]
    s2 = lax.optimization_barrier(s2).reshape(freqs, sources * k, bins).transpose(0, 2, 1)
    table = lag_table(freqs * bins).reshape(2, freqs, PARTS, width, LAGS).transpose(4, 2, 1, 0, 3)
    table = jnp.asarray(table.reshape(LAGS, 2 * freqs * bins), jnp.bfloat16)
    picks = jnp.asarray(spread_table(sources, k), jnp.bfloat16)
    dma = pltpu.SemaphoreType.DMA
    vmem = pl.BlockSpec(memory_space=pltpu.VMEM)
    bf16, f32 = jnp.bfloat16, jnp.float32
    return pl.pallas_call(
        functools.partial(kernel, depth, ring, windows),
        out_shape=jax.ShapeDtypeStruct((ROUNDS, sources, channels, LAGS), f32),
        in_specs=[pl.BlockSpec(memory_space=pltpu.SMEM), vmem, vmem, vmem, vmem],
        out_specs=vmem,
        scratch_shapes=[
            pltpu.VMEM((8 + freqs, channels), f32),
            pltpu.VMEM((freqs, 8 + freqs, channels), f32),
            pltpu.VMEM((8 + freqs, channels), f32),
            pltpu.VMEM((groups, 8, channels), f32),
            pltpu.VMEM((ROUNDS + 1, 8, channels), f32),
            pltpu.VMEM(s2.shape, bf16),
            pltpu.VMEM((PARTS, ROUNDS, depth, rows, k, channels), bf16),
            pltpu.VMEM((PARTS, freqs, ROUNDS, width, k, channels), bf16),
            pltpu.VMEM((freqs * bins // 16, 2 * sources, 16, 16 * k), bf16),
            pltpu.VMEM((sources, 2 * width * freqs, ROUNDS * channels), bf16),
            pltpu.VMEM((sources, LAGS, ROUNDS * channels), f32),
        ]
        + [pltpu.VMEM((groups, rows, k, channels), bf16)] * PARTS
        + [
            dma((freqs,)), dma((freqs,)),
            dma((depth,)), dma((depth,)),
            dma((3,)), dma((3,)),
            dma((freqs,)), dma((freqs,)),
            dma((PARTS, depth)), dma((PARTS, depth)),
            dma((PARTS, depth // BATCH)), dma((PARTS, depth // BATCH)),
            dma((PARTS, 2, depth // BATCH)), dma((PARTS, 2, depth // BATCH)),
            dma((PARTS, ROUNDS, depth)), dma((PARTS, ROUNDS, depth)),
            dma((PARTS, ROUNDS, 9)), dma((PARTS, ROUNDS, 9)),
        ],
        compiler_params=pltpu.CompilerParams(
            collective_id=0, has_side_effects=True, vmem_limit_bytes=48 * 2**20
        ),
        name="correlate_pairs",
    )(pairing, x, s2, table, picks)


def solution(mesh):
    placed = (P("grp", None, None, "freq"), P())
    return jax.shard_map(
        functools.partial(per_device, dict(mesh.shape)),
        mesh=mesh,
        in_specs=placed,
        out_specs=P(None, ("grp", "freq"), None, None),
        check_vma=False,
    )
```

```python
import functools
import math

import jax
import jax.numpy as jnp
import numpy as np
from jax import lax
from jax.experimental import pallas as pl
from jax.experimental.pallas import tpu as pltpu
from jax.sharding import PartitionSpec as P

LAGS = 256
VIRTUAL_SOURCES = 64
ROUNDS = 2
MESH = pl.DeviceIdType.MESH
PARTS = 4
BATCH = 8
Y_FIRST = ((0, 1), (1, 1), (2, 1))
ORDER = (
    ("E0", "Z1", "P0", "Z2", "E1", "Q0", "E2", "R0", "X0", "P1", "Q1", "R1", "X1", "O0", "E3", "W0")
    + ("F0", "X2", "P2", "Q2", "W1", "Z3", "F1", "S0", "X3", "R2", "F2", "X4", "S1", "T0", "P3", "Q3")
    + ("F3", "X5", "S2", "T1", "U0", "R3", "F4", "X6", "S3", "T2", "U1", "L0", "F5", "X7", "S4", "T3")
    + ("U2", "L1", "A0", "F6", "S5", "B0", "T4", "U3", "G0", "L2", "F7", "S6", "T5", "U4", "L3", "S7")
    + ("A1", "T6", "B1", "U5", "G1", "L4", "T7", "U6", "L5", "A2", "B2", "G2", "A3", "U7", "L6", "L7")
    + ("B3", "G3", "z0", "z1", "z2", "z3", "s0", "s1", "s2", "s3", "s4", "s5", "s6", "s7")
)


def lag_table(freq_total):
    bins = np.arange(freq_total)
    shifts = np.arange(LAGS) - LAGS // 2
    theta = (bins[:, None] * shifts[None, :] % (2 * freq_total)) * (math.pi / freq_total)
    weights = np.where(bins == 0, 1.0, 2.0) / (2.0 * freq_total)
    return np.stack([weights[:, None] * np.cos(theta), -weights[:, None] * np.sin(theta)])


def spread_table(sources, k):
    table = np.zeros((sources, k, sources, 2, 16, k), np.float32)
    for s in range(sources):
        for w in range(k // 2):
            table[s, 2 * w, s, 0, :, 2 * w] = 1.0
            table[s, 2 * w + 1, s, 0, :, 2 * w + 1] = 1.0
            table[s, 2 * w + 1, s, 1, :, 2 * w] = 1.0
            table[s, 2 * w, s, 1, :, 2 * w + 1] = -1.0
    return table.reshape(sources * k, sources * 2 * 16 * k)


def kernel(
    depth, ring, windows,
    pair, x, s2, table, picks, out,
    e_own, e_all, e_sum, e_grp, norm, s2o, send, blk, w, spec, acc, *rest,
):
    mids = rest[:PARTS]
    (e_ss, e_rs, g_ss, g_rs, t_ss, t_rs, s_ss, s_rs, z_ss, z_rs, l_ss, l_rs, c_ss, c_rs, p_ss, p_rs, a_ss, a_rs) = rest[PARTS:]
    freqs = 2 * ring
    bins, k, channels = x.shape
    width = bins // PARTS
    rows = width // depth
    sources = out.shape[1]
    wide = 16 * k
    tiles = width // 16
    g = lax.axis_index("grp")
    q = lax.axis_index("freq")
    z = lax.div(g, 4)
    quad = lax.rem(g, 4)
    lo = lax.div(quad, 2)
    core = lax.rem(quad, 2)
    y = lax.div(q, 2)
    hi = lax.rem(q, 2)
    up = lax.rem(y + 1, ring)
    down = lax.rem(y + ring - 1, ring)
    across = lax.rem(y + 2, ring)
    lo_quad = (1 - lo) * 2 + core
    core_quad = lo * 2 + 1 - core
    far_quad = (1 - lo) * 2 + 1 - core
    lo_dev = (z * 4 + lo_quad, q)
    core_dev = (z * 4 + core_quad, q)
    mate = y * 2 + 1 - hi
    mate_dev = (g, mate)
    up_dev = (g, up * 2 + hi)
    down_dev = (g, down * 2 + hi)

    def z_dev(zt):
        return (zt * 4 + quad, q)

    def place(i):
        d = lax.div(i + 1, 2)
        return lax.rem(z + i, depth)

    def copy(src, dst, ss, rs, dev):
        pltpu.make_async_remote_copy(
            src_ref=src, dst_ref=dst, send_sem=ss, recv_sem=rs, device_id=dev, device_id_type=MESH
        ).start()

    def arrived(ref, sem):
        pltpu.make_async_copy(ref, ref, sem).wait()

    barrier = pltpu.get_barrier_semaphore()
    for d in range(1, depth):
        pl.semaphore_signal(barrier, inc=1, device_id=z_dev(lax.rem(z + d, depth)), device_id_type=MESH)
    for d in range(1, freqs):
        pl.semaphore_signal(barrier, inc=1, device_id=(g, lax.rem(q + d, freqs)), device_id_type=MESH)
    for dev in (lo_dev, core_dev):
        pl.semaphore_signal(barrier, inc=1, device_id=dev, device_id_type=MESH)

    def square_sum(i, total):
        v = x[pl.ds(i * 8, 8)].astype(jnp.float32)
        return total + jnp.sum(v * v, axis=0)

    total = lax.fori_loop(0, bins // 8, square_sum, jnp.zeros((k, channels), jnp.float32))
    e_own[0:8] = jnp.broadcast_to(jnp.sum(total, axis=0, keepdims=True), (8, channels))
    for i in range(freqs):
        v = s2[i].astype(jnp.float32)
        e_own[8 + i : 9 + i] = jnp.sum(v * v, axis=0, keepdims=True)
    lanes = e_own.shape[1]
    same = lax.div(lax.broadcasted_iota(jnp.int32, (lanes, lanes), 0), k) == lax.div(
        lax.broadcasted_iota(jnp.int32, (lanes, lanes), 1), k
    )
    e_own[8:] = jnp.dot(
        e_own[8:], same.astype(jnp.float32), precision=lax.Precision.HIGHEST, preferred_element_type=jnp.float32
    )

    pl.semaphore_wait(barrier, depth - 1 + freqs - 1 + 2)

    def spread(a):
        def step(i, carry):
            zt = place(i)
            copy(
                x.at[pl.ds(a * width + zt * rows, rows)], mids[a].at[quad * depth + z],
                z_ss.at[a, zt], z_rs.at[a, z], z_dev(zt),
            )
            return carry

        lax.fori_loop(1, depth, step, 0)
        mids[a][pl.ds(quad * depth + z, 1)] = x[pl.ds(a * width + z * rows, rows)][None]

    spread(0)
    for d in range(1, freqs):
        to = lax.rem(q + d, freqs)
        copy(e_own, e_all.at[q], e_ss.at[d], e_rs.at[q], (g, to))
    e_all[q] = e_own[...]
    for d in range(1, freqs):
        to = lax.rem(q + d, freqs)
        copy(s2.at[to], s2o.at[q], s_ss.at[d], s_rs.at[q], (g, to))
    s2o[q] = s2[q]

    def energy_run(quarter):
        return e_grp.at[pl.ds(quarter * depth, depth)]

    def energies(step):
        if step == 0:
            for d in range(1, freqs):
                src = lax.rem(q + d, freqs)
                arrived(e_all.at[src], e_rs.at[src])
            total = e_all[0]
            for i in range(1, freqs):
                total = total + e_all[i]
            e_sum[...] = total
            e_grp[quad * depth + z] = total[0:8]

            def one(i, carry):
                zt = place(i)
                copy(e_sum.at[pl.ds(0, 8)], e_grp.at[quad * depth + z], g_ss.at[zt], g_rs.at[z], z_dev(zt))
                return carry

            lax.fori_loop(1, depth, one, 0)
        if step == 1:
            def one(d, carry):
                zs = lax.rem(z + d, depth)
                arrived(e_grp.at[quad * depth + zs], g_rs.at[zs])
                return carry

            lax.fori_loop(1, depth, one, 0)
            copy(energy_run(quad), energy_run(quad), t_ss.at[0], t_rs.at[0], lo_dev)
            copy(energy_run(quad), energy_run(quad), t_ss.at[1], t_rs.at[1], core_dev)
        if step == 2:
            arrived(energy_run(lo_quad), t_rs.at[0])
            copy(energy_run(lo_quad), energy_run(lo_quad), t_ss.at[2], t_rs.at[2], core_dev)
        if step == 3:
            arrived(energy_run(core_quad), t_rs.at[1])
            arrived(energy_run(far_quad), t_rs.at[2])
            count = k * bins * freqs
            for r in range(ROUNDS):
                p = pair[r, g]
                norm[r] = lax.rsqrt(e_grp[lax.rem(p, 4) * depth + lax.div(p, 4)] / count + 1e-06)
            own = e_sum[pl.ds(8 + q, 1)]
            norm[ROUNDS] = jnp.broadcast_to(lax.rsqrt(own / count + 1e-06), (8, channels))

    batches = depth // BATCH

    def run(a, quarter, b):
        return mids[a].at[pl.ds(quarter * depth + b * BATCH, BATCH)]

    def pass_on(a):
        def step(i, carry):
            b = lax.rem(lax.div(z, BATCH) + i, batches)

            def one(j, carry):
                zs = b * BATCH + j

                @pl.when(zs != z)
                def _():
                    arrived(mids[a].at[quad * depth + zs], z_rs.at[a, zs])

                return carry

            lax.fori_loop(0, BATCH, one, 0)
            part = run(a, quad, b)
            copy(part, part, l_ss.at[a, b], l_rs.at[a, b], lo_dev)
            copy(part, part, c_ss.at[a, 0, b], c_rs.at[a, 0, b], core_dev)
            return carry

        lax.fori_loop(0, batches, step, 0)

    def pass_twice(a):
        def step(i, carry):
            b = lax.rem(lax.div(z, BATCH) + i, batches)
            part = run(a, lo_quad, b)
            arrived(part, l_rs.at[a, b])
            copy(part, part, c_ss.at[a, 1, b], c_rs.at[a, 1, b], core_dev)
            return carry

        lax.fori_loop(0, batches, step, 0)

    def passed(a):
        for b in range(batches):
            arrived(run(a, core_quad, b), c_rs.at[a, 0, b])
            arrived(run(a, far_quad, b), c_rs.at[a, 1, b])

    def select(a, r):
        here = pl.ds(z * rows, rows)

        def wanted(zt):
            p = pair[r, zt * 4 + quad]
            return mids[a][lax.rem(p, 4) * depth + lax.div(p, 4)]

        def step(i, carry):
            zt = place(i)
            send[a, r, zt] = wanted(zt)
            copy(send.at[a, r, zt], blk.at[a, q, r, here], p_ss.at[a, r, zt], p_rs.at[a, r, z], z_dev(zt))
            return carry

        lax.fori_loop(1, depth, step, 0)
        blk[a, q, r, here] = wanted(z)

    half = width // 2

    def block(a, r, fb):
        return blk.at[a, fb, r]

    def halves(a, r, fb, h):
        return blk.at[a, fb, r, pl.ds(h * half, half)]

    def ship(ref, a, r, i, dev):
        copy(ref, ref, a_ss.at[a, r, i], a_rs.at[a, r, i], dev)

    def first(a, r):
        def one(d, carry):
            zm = lax.rem(z + d, depth)
            arrived(blk.at[a, q, r, pl.ds(zm * rows, rows)], p_rs.at[a, r, zm])
            return carry

        lax.fori_loop(1, depth, one, 0)
        own = block(a, r, q)
        if (a, r) not in Y_FIRST:
            ship(own, a, r, 0, mate_dev)
        ship(own, a, r, 1, up_dev)
        ship(own, a, r, 3, down_dev)
        if (a, r) in Y_FIRST:
            ship(own, a, r, 0, mate_dev)

    def second(a, r):
        if (a, r) in Y_FIRST:
            return
        other = block(a, r, mate)
        arrived(other, a_rs.at[a, r, 0])
        ship(other, a, r, 2, up_dev)
        ship(other, a, r, 4, down_dev)

    def third(a, r):
        for i in range(1 if (a, r) in Y_FIRST else 2):
            side = hi if i == 0 else 1 - hi
            low, high = down * 2 + side, up * 2 + side
            arrived(block(a, r, low), a_rs.at[a, r, 1 + i])
            ship(halves(a, r, low, 0), a, r, 5 + i, up_dev)
            arrived(block(a, r, high), a_rs.at[a, r, 3 + i])
            ship(halves(a, r, high, 1), a, r, 7 + i, down_dev)
            if (a, r) in Y_FIRST:
                ship(block(a, r, low), a, r, 2, mate_dev)
                ship(block(a, r, high), a, r, 4, mate_dev)

    def fourth(a, r):
        if (a, r) in Y_FIRST:
            arrived(halves(a, r, across * 2 + hi, 0), a_rs.at[a, r, 5])
            arrived(halves(a, r, across * 2 + hi, 1), a_rs.at[a, r, 7])
            ship(block(a, r, across * 2 + hi), a, r, 6, mate_dev)
            return
        for i in range(2):
            side = hi if i == 0 else 1 - hi
            arrived(halves(a, r, across * 2 + side, 0), a_rs.at[a, r, 5 + i])
            arrived(halves(a, r, across * 2 + side, 1), a_rs.at[a, r, 7 + i])

    def last(a, r):
        if (a, r) in Y_FIRST:
            arrived(block(a, r, mate), a_rs.at[a, r, 0])
            arrived(block(a, r, down * 2 + 1 - hi), a_rs.at[a, r, 2])
            arrived(block(a, r, up * 2 + 1 - hi), a_rs.at[a, r, 4])
            arrived(block(a, r, across * 2 + 1 - hi), a_rs.at[a, r, 6])

    def weights(part):
        row = lax.broadcasted_iota(jnp.int32, (16, wide), 0)
        col = lax.broadcasted_iota(jnp.int32, (16, wide), 1)
        mask = lax.div(col, k) == row
        near = freqs // 2

        def step(i, carry):
            at = pl.ds(i * near, near)
            v = s2o[at].astype(jnp.float32) * norm[ROUNDS, 0:1][None]
            v = v.astype(jnp.bfloat16).reshape(near * bins, sources * k)
            for n in range(part * sources, (part + 1) * sources):
                u = jnp.dot(v, picks[:, n * wide : (n + 1) * wide], preferred_element_type=jnp.float32)
                u = jnp.where(mask[None], u.reshape(near * bins // 16, 16, wide), 0.0).astype(jnp.bfloat16)
                w[pl.ds(i * near * bins // 16, near * bins // 16), n] = u
            return carry

        lax.fori_loop(0, freqs // near, step, 0)

    def spectra(a, row):
        def step(side, carry):
            fb = row * 2 + side
            for t in range(tiles):
                right = jnp.concatenate(
                    [
                        (blk[a, fb, r, t * 16 : (t + 1) * 16].astype(jnp.float32) * norm[r, 0:1][None])
                        .astype(jnp.bfloat16)
                        .reshape(wide, channels)
                        for r in range(ROUNDS)
                    ],
                    axis=1,
                )
                left = w[fb * (bins // 16) + a * tiles + t].reshape(2 * sources * 16, wide)
                v = jnp.dot(left, right, preferred_element_type=jnp.float32)
                v = (v * (1.0 / windows)).astype(jnp.bfloat16)
                for s in range(sources):
                    for part in range(2):
                        n = s * 2 + part
                        at = pl.multiple_of(fb * (2 * width) + part * width + t * 16, 16)
                        spec[s, pl.ds(at, 16), :] = v[n * 16 : (n + 1) * 16]
            return carry

        lax.fori_loop(0, 2, step, 0)

    def near_spectra(a):
        for row in (y, up, down):
            spectra(a, row)

    def lags_of(a):
        span = 2 * width * freqs

        def lags(s, carry):
            v = jnp.dot(table[:, a * span : (a + 1) * span], spec[s], preferred_element_type=jnp.float32)
            if a > 0:
                v = v + acc[s]
            if a == PARTS - 1:
                for r in range(ROUNDS):
                    out[r, s] = v[:, r * channels : (r + 1) * channels].T
            else:
                acc[s] = v
            return carry

        lax.fori_loop(0, sources, lags, 0)

    turns = [(a, r) for a in range(PARTS) for r in range(ROUNDS)]

    def spread_sent(a):
        def one(d, carry):
            arrived(mids[a].at[0], z_ss.at[a, lax.rem(z + d, depth)])
            return carry

        lax.fori_loop(1, depth, one, 0)

    def select_sent(a, r):
        def one(d, carry):
            arrived(mids[a].at[0], p_ss.at[a, r, lax.rem(z + d, depth)])
            return carry

        lax.fori_loop(1, depth, one, 0)

    def sources_here():
        for d in range(1, freqs):
            src = lax.rem(q + d, freqs)
            arrived(s2o.at[src], s_rs.at[src])

    names = {
        "z": lambda a: spread_sent(a),
        "s": lambda t: select_sent(*turns[t]),
        "Z": lambda a: spread(a),
        "P": lambda a: pass_on(a),
        "Q": lambda a: pass_twice(a),
        "R": lambda a: passed(a),
        "X": lambda t: select(*turns[t]),
        "F": lambda t: first(*turns[t]),
        "S": lambda t: second(*turns[t]),
        "T": lambda t: third(*turns[t]),
        "U": lambda t: fourth(*turns[t]),
        "L": lambda t: last(*turns[t]),
        "O": lambda a: sources_here(),
        "W": lambda a: weights(a),
        "A": lambda a: near_spectra(a),
        "B": lambda a: spectra(a, across),
        "G": lambda a: lags_of(a),
        "E": lambda a: energies(a),
    }
    for name in ORDER:
        names[name[0]](int(name[1]))

    for d in range(1, freqs):
        arrived(s2.at[0], s_ss.at[d])
        arrived(e_own, e_ss.at[d])

    def energy_sent(d, carry):
        arrived(e_grp.at[0], g_ss.at[lax.rem(z + d, depth)])
        return carry

    lax.fori_loop(1, depth, energy_sent, 0)
    for i in range(3):
        arrived(energy_run(0), t_ss.at[i])
    for a in range(PARTS):
        for b in range(batches):
            arrived(run(a, 0, b), l_ss.at[a, b])
            arrived(run(a, 0, b), c_ss.at[a, 0, b])
            arrived(run(a, 0, b), c_ss.at[a, 1, b])
        for r in range(ROUNDS):
            y_first = (a, r) in Y_FIRST
            for i in range(9):
                if y_first and i == 8:
                    continue
                whole = i < 5 or (y_first and i == 6)
                arrived(block(a, r, 0) if whole else halves(a, r, 0, 0), a_ss.at[a, r, i])


def per_device(mesh_shape, spectra, pairing):
    channels, windows, two, bins = spectra.shape
    freqs, groups = mesh_shape["freq"], mesh_shape["grp"]
    depth, ring = groups // 4, freqs // 2
    k = windows * two
    sources = VIRTUAL_SOURCES // freqs
    width = bins // PARTS
    rows = width // depth
    step = channels // VIRTUAL_SOURCES
    x = spectra.reshape(channels, k, bins).transpose(2, 1, 0)
    s2 = spectra.reshape(VIRTUAL_SOURCES, step, k, bins)[:, 0]
    s2 = lax.optimization_barrier(s2).reshape(freqs, sources * k, bins).transpose(0, 2, 1)
    table = lag_table(freqs * bins).reshape(2, freqs, PARTS, width, LAGS).transpose(4, 2, 1, 0, 3)
    table = jnp.asarray(table.reshape(LAGS, 2 * freqs * bins), jnp.bfloat16)
    picks = jnp.asarray(spread_table(sources, k), jnp.bfloat16)
    dma = pltpu.SemaphoreType.DMA
    vmem = pl.BlockSpec(memory_space=pltpu.VMEM)
    bf16, f32 = jnp.bfloat16, jnp.float32
    return pl.pallas_call(
        functools.partial(kernel, depth, ring, windows),
        out_shape=jax.ShapeDtypeStruct((ROUNDS, sources, channels, LAGS), f32),
        in_specs=[pl.BlockSpec(memory_space=pltpu.SMEM), vmem, vmem, vmem, vmem],
        out_specs=vmem,
        scratch_shapes=[
            pltpu.VMEM((8 + freqs, channels), f32),
            pltpu.VMEM((freqs, 8 + freqs, channels), f32),
            pltpu.VMEM((8 + freqs, channels), f32),
            pltpu.VMEM((groups, 8, channels), f32),
            pltpu.VMEM((ROUNDS + 1, 8, channels), f32),
            pltpu.VMEM(s2.shape, bf16),
            pltpu.VMEM((PARTS, ROUNDS, depth, rows, k, channels), bf16),
            pltpu.VMEM((PARTS, freqs, ROUNDS, width, k, channels), bf16),
            pltpu.VMEM((freqs * bins // 16, 2 * sources, 16, 16 * k), bf16),
            pltpu.VMEM((sources, 2 * width * freqs, ROUNDS * channels), bf16),
            pltpu.VMEM((sources, LAGS, ROUNDS * channels), f32),
        ]
        + [pltpu.VMEM((groups, rows, k, channels), bf16)] * PARTS
        + [
            dma((freqs,)), dma((freqs,)),
            dma((depth,)), dma((depth,)),
            dma((3,)), dma((3,)),
            dma((freqs,)), dma((freqs,)),
            dma((PARTS, depth)), dma((PARTS, depth)),
            dma((PARTS, depth // BATCH)), dma((PARTS, depth // BATCH)),
            dma((PARTS, 2, depth // BATCH)), dma((PARTS, 2, depth // BATCH)),
            dma((PARTS, ROUNDS, depth)), dma((PARTS, ROUNDS, depth)),
            dma((PARTS, ROUNDS, 9)), dma((PARTS, ROUNDS, 9)),
        ],
        compiler_params=pltpu.CompilerParams(
            collective_id=0, has_side_effects=True, vmem_limit_bytes=48 * 2**20
        ),
        name="correlate_pairs",
    )(pairing, x, s2, table, picks)


def solution(mesh):
    placed = (P("grp", None, None, "freq"), P())
    return jax.shard_map(
        functools.partial(per_device, dict(mesh.shape)),
        mesh=mesh,
        in_specs=placed,
        out_specs=P(None, ("grp", "freq"), None, None),
        check_vma=False,
    )
```
